32 devices in a mesh: dp: 8 (over z, x), mp: 4 (over y, core).
Axes of the slice: x: 2, y: 2, z: 4, core: 2. Of those that a mesh axis runs over, the one named last changes fastest.
Arguments:
- preactivation: bfloat16 [3584, 32768], P('dp', 'mp'), may hold values from -6 to 6
- upstream: bfloat16 [3584, 512], P('dp'), may hold values from -0.29882812 to 0.29882812
- weight: bfloat16 [32768, 512], P('mp'), may hold values from -40 to 40
- first_moment: float32 [32768, 512], P(('mp', 'dp')), may hold values from -4 to 4
- second_moment: float32 [32768, 512], P(('mp', 'dp')), may hold values from 1 to 16
Outputs:
- input_grad: bfloat16 [3584, 32768], P('dp', 'mp')
- new_weight: bfloat16 [32768, 512], P('mp')
- first_next: float32 [32768, 512], P(('mp', 'dp'))
- second_next: float32 [32768, 512], P(('mp', 'dp'))
- trust_step: float32 [32768, 512], P(('mp', 'dp'))
The draws below stay inside these ranges and needn't reach their ends.
All inputs are finite; a program needn't handle non-finite values.
Results may differ from the reference program's by a relative error of at most 0.015.
Values may be sent and summed in bfloat16 or wider, within the bound.
A program may use at most 128 MiB of HBM per device.

```python
import math
import jax
import jax.numpy as jnp
from jax import lax

D = 512
FF = 32768
TOK_DEV = 448
STEP = 1000
TOKENS = 3584
N_DP = 8


def draw_weight(key, part):
    key = jax.random.fold_in(key, 11)
    key_base, key_rows, key_cols = jax.random.split(key, 3)
    position = jnp.arange(FF, dtype=jnp.float32) / (FF - 1)
    base = jax.random.truncated_normal(key_base, -4.0, 4.0, (FF, D), jnp.float32)
    rising = 3.0 ** (0.5 * position)
    row_spread = jnp.exp(jax.random.uniform(key_rows, (FF, 1), jnp.float32, -1.15, 1.15))
    col_spread = jnp.exp(jax.random.uniform(key_cols, (1, D), jnp.float32, -0.5, 0.5))
    return (base * rising[:, None] * row_spread * col_spread).astype(jnp.bfloat16)


def with_spikes(values, key, source, target, parts, factor):
    owner, partner = [(jnp.arange(values.shape[dim]) // (values.shape[dim] // parts)).reshape([-1 if axis == dim else 1 for axis in range(values.ndim)]) for dim in (source, target)]
    chosen = jax.random.permutation(key, parts)[partner]
    strong = (owner == chosen) | (owner == (partner + parts // 2) % parts)
    return jnp.where(strong, factor * values, values)


def steps_of(stream_key, extent, cuts, smallest, largest):
    def one(dim, shards_of):
        draws = jax.random.uniform(jax.random.fold_in(jax.random.fold_in(stream_key, 6), dim), (shards_of,), jnp.float32, smallest / len(cuts), largest / len(cuts))
        return jnp.repeat(jnp.exp(draws), extent[dim] // shards_of).reshape((-1,) + (1,) * (len(extent) - dim - 1))

    factor_of = one(*cuts[0])
    for cut in cuts[1:]:
        factor_of = factor_of * one(*cut)
    return factor_of


def noise(rng, dims, scale, bound, cuts=(), kind=jnp.bfloat16):
    values = scale * jax.random.normal(rng, dims, jnp.float32)
    if cuts:
        values = values * steps_of(rng, dims, cuts, -0.22, 0.18)
    return jnp.clip(values, -bound, bound).astype(kind)


def noise_with(own_key, extent, width, reach, cuts, heavy, kind=jnp.bfloat16):
    values = width * jax.random.normal(own_key, extent, jnp.float32)
    if cuts:
        values = values * steps_of(own_key, extent, cuts, -0.22, 0.18)
    return jnp.clip(with_spikes(values, jax.random.fold_in(own_key, 3), *heavy), -reach, reach).astype(kind)


def setup_inputs(seed: int = 0) -> dict:
    key_of = jax.random.split(jax.random.key(seed), 6)
    preactivation = noise_with(key_of[0], (TOKENS, FF), 1.0, 6.0, ((0, 8), (1, 4)), (0, 1, 8, 2.0))
    upstream = noise(key_of[1], (TOKENS, D), 0.044, 0.29882812, ((0, 8),))
    weight = draw_weight(jax.random.fold_in(key_of[5], 71), 0)
    first_moment = noise(key_of[3], (FF, D), 0.5, 4.0, ((0, 32),), jnp.float32)
    second_moment = jnp.clip(jnp.exp(math.log(16.0) - 2.7725887 * jax.random.uniform(key_of[4], (FF, D), jnp.float32) ** steps_of(key_of[4], (FF, D), ((0, 32),), -0.2, 0.2)), 1.0, 16.0)
    return dict(preactivation=preactivation, upstream=upstream, weight=weight, first_moment=first_moment, second_moment=second_moment)


def reference(preactivation, upstream, weight, first_moment, second_moment):
    hidden = jnp.maximum(preactivation, jnp.zeros((), jnp.bfloat16))
    pre_blocks = preactivation.reshape(N_DP, TOK_DEV, FF)
    hid_blocks = hidden.reshape(N_DP, TOK_DEV, FF)
    up_blocks = upstream.reshape(N_DP, TOK_DEV, D)

    def one_block(total, items):
        pre_block, hid_block, up_block = items
        back = jnp.dot(up_block, weight.T, preferred_element_type=jnp.float32)
        grad_block = jnp.where(pre_block > 0, back, jnp.zeros((), jnp.float32)).astype(jnp.bfloat16)
        partial_value = jnp.dot(hid_block.T, up_block, preferred_element_type=jnp.float32).astype(jnp.bfloat16)
        partial_value = lax.optimization_barrier(partial_value)
        return (total + partial_value.astype(jnp.float32), grad_block)
    gradient, grad_blocks = lax.scan(one_block, jnp.zeros((FF, D), jnp.float32), (pre_blocks, hid_blocks, up_blocks))
    input_grad = grad_blocks.reshape(N_DP * TOK_DEV, FF)
    beta_one = 0.9
    beta_two = 0.999
    bias_one = 1.0 - beta_one ** STEP
    bias_two = 1.0 - beta_two ** STEP
    first_next = beta_one * first_moment + (1.0 - beta_one) * gradient
    second_next = beta_two * second_moment + (1.0 - beta_two) * gradient * gradient
    weight_full = weight.astype(jnp.float32)
    update = first_next / bias_one / (jnp.sqrt(second_next / bias_two) + 1e-06) + 0.02 * weight_full
    weight_sq = jnp.sum(weight_full * weight_full)
    update_sq = jnp.sum(update * update)
    trust_step = jnp.sqrt(weight_sq) / jnp.sqrt(update_sq) * update
    new_weight = (weight_full - 0.02 * trust_step).astype(jnp.bfloat16)
    return (input_grad, new_weight, first_next, second_next, trust_step)
```

```python
import functools

import jax
import jax.numpy as jnp
from jax import lax
from jax.experimental import pallas as pl
from jax.experimental.pallas import tpu as pltpu
from jax.sharding import PartitionSpec as P

STEP = 1000
BETA_ONE = 0.9
BETA_TWO = 0.999
BIAS_ONE = 1.0 - BETA_ONE**STEP
BIAS_TWO = 1.0 - BETA_TWO**STEP
MESH = pl.DeviceIdType.MESH


def moments(gradient, first_moment, second_moment, own_weight):
    first_next = BETA_ONE * first_moment + (1.0 - BETA_ONE) * gradient
    second_next = BETA_TWO * second_moment + (1.0 - BETA_TWO) * gradient * gradient
    update = first_next / BIAS_ONE / (jnp.sqrt(second_next / BIAS_TWO) + 1e-06) + 0.02 * own_weight
    return first_next, second_next, update


def kernel(
    nz, nmp, chunks, lag,
    pre, ups, w_hbm, m, v,
    g_out, upd, nrm,
    xs, xr, zb, ub, wv, acc, nsend, nrecv,
    xs_s, xr_s, zs_s, zr_s, ax_s, az_s, ar_s, own_s, w_s, ns_s, nr_s,
):
    dp = lax.axis_index("dp")
    mp = lax.axis_index("mp")
    z, x = dp // 2, dp % 2
    rows = m.shape[0]
    part = rows // chunks
    steps = nz * chunks
    partner = 2 * z + 1 - x
    below, above = dp - 2, dp + 2

    flips = []
    bit = 1
    while bit < 2 * nz:
        flips.append({"dp": dp + bit * (1 - 2 * ((dp // bit) % 2))})
        bit *= 2
    bit = 1
    while bit < nmp:
        flips.append({"mp": mp + bit * (1 - 2 * ((mp // bit) % 2))})
        bit *= 2

    w_copy = pltpu.make_async_copy(
        w_hbm.at[pl.ds(pl.multiple_of(dp * rows, rows), rows)], wv, w_s
    )
    w_copy.start()

    barrier = pltpu.get_barrier_semaphore()
    for k, device in enumerate(flips):
        if k != 1:
            pl.semaphore_signal(barrier, inc=1, device_id=device, device_id_type=MESH)

    @pl.when(z > 0)
    def _():
        pl.semaphore_signal(barrier, inc=1, device_id={"dp": below}, device_id_type=MESH)

    @pl.when(z < nz - 1)
    def _():
        pl.semaphore_signal(barrier, inc=1, device_id={"dp": above}, device_id_type=MESH)

    ends = jnp.where(z > 0, 1, 0) + jnp.where(z < nz - 1, 1, 0)
    pl.semaphore_wait(barrier, len(flips) - 1 + ends)

    def order(j):
        up, down = nz - 1 - z, z
        short = jnp.minimum(up, down)
        single = nz - 1 - 2 * short
        toward = jnp.where(up >= down, 1, -1)
        t = jnp.maximum(j - single, 0)
        dist = jnp.where(j < single, jnp.maximum(up, down) - j, short - t // 2)
        side = jnp.where(j < single, 1, 1 - 2 * (t % 2))
        return z + toward * side * dist

    def partial_of(dest, column, c):
        at = pl.multiple_of((2 * dest + column) * rows + c * part, part)
        hidden = jnp.maximum(pre[:, pl.ds(at, part)], jnp.zeros((), jnp.bfloat16))
        return lax.dot_general(
            hidden, ups[...], (((0,), (0,)), ((), ())), preferred_element_type=jnp.float32
        )

    def remote(src, dst, send, recv, device):
        return pltpu.make_async_remote_copy(
            src_ref=src, dst_ref=dst, send_sem=send, recv_sem=recv,
            device_id={"dp": device}, device_id_type=MESH,
        )

    def x_copy(k):
        return remote(xs.at[k], xr.at[k], xs_s.at[k], xr_s.at[k], partner)

    def z_copy(way, k, device):
        at = way * steps + k
        return remote(zb.at[at], zb.at[at], zs_s.at[at], zr_s.at[at], device)

    def shard_rows(shard, c):
        return pl.ds(pl.multiple_of(shard * rows + c * part, part), part)

    def own_rows(c):
        return pl.ds(pl.multiple_of(c * part, part), part)

    def ag_copy(src, place, c, send, device, column):
        at = shard_rows(2 * place + column, c)
        recv = ar_s.at[(2 * place + column) * chunks + c]
        return remote(src, upd.at[at], send, recv, device)

    def own_copy(c):
        return pltpu.make_async_copy(
            ub.at[own_rows(c)], upd.at[shard_rows(dp, c)], own_s.at[c]
        )

    def send_x(t, carry):
        c, dest = t // nz, order(t % nz)
        k = c * nz + dest
        xs[k] = partial_of(dest, 1 - x, c).astype(jnp.bfloat16)
        x_copy(k).start()
        return carry

    lax.fori_loop(0, steps, send_x, 0)
    w_copy.wait()
    acc[...] = jnp.zeros_like(acc)

    def rs_step(t):
        c, dest = t // nz, order(t % nz)
        k = c * nz + dest
        total = partial_of(dest, x, c)
        x_copy(k).wait_recv()
        total = total + xr[k].astype(jnp.float32)
        g_out[own_rows(c)] = total

        @pl.when((dest >= z) & (z > 0))
        def _():
            z_copy(0, k, below).wait_recv()
            g_out[own_rows(c)] += zb[k].astype(jnp.float32)

        @pl.when((dest <= z) & (z < nz - 1))
        def _():
            z_copy(1, k, above).wait_recv()
            g_out[own_rows(c)] += zb[steps + k].astype(jnp.float32)

        @pl.when(dest > z)
        def _():
            zb[k] = g_out[own_rows(c)].astype(jnp.bfloat16)
            z_copy(0, k, above).start()

        @pl.when(dest < z)
        def _():
            zb[steps + k] = g_out[own_rows(c)].astype(jnp.bfloat16)
            z_copy(1, k, below).start()

        @pl.when(dest == z)
        def _():
            own_weight = wv[own_rows(c)].astype(jnp.float32)
            _, _, update = moments(g_out[own_rows(c)], m[own_rows(c)], v[own_rows(c)], own_weight)
            ub[own_rows(c)] = update.astype(jnp.bfloat16)
            own_copy(c).start()
            acc[0:1] += jnp.sum(own_weight * own_weight, axis=0, keepdims=True)
            acc[1:2] += jnp.sum(update * update, axis=0, keepdims=True)

    def ag_sends(t, act):
        c, place = t // nz, order(nz - 1 - t % nz)
        k = c * nz + place

        @pl.when(place == z)
        def _():
            src = ub.at[own_rows(c)]

            @pl.when(z < nz - 1)
            def _():
                act(ag_copy(src, place, c, az_s.at[k], above, x))

            @pl.when(z > 0)
            def _():
                act(ag_copy(src, place, c, az_s.at[steps + k], below, x))

            act(ag_copy(src, place, c, ax_s.at[k], partner, x))

        @pl.when(place != z)
        def _():
            src = upd.at[shard_rows(2 * place + x, c)]

            @pl.when((place < z) & (z < nz - 1))
            def _():
                act(ag_copy(src, place, c, az_s.at[k], above, x))

            @pl.when((place > z) & (z > 0))
            def _():
                act(ag_copy(src, place, c, az_s.at[steps + k], below, x))

            act(ag_copy(src, place, c, ax_s.at[k], partner, x))

    def ag_step(t):
        c, place = t // nz, order(nz - 1 - t % nz)

        @pl.when(place != z)
        def _():
            src = upd.at[shard_rows(2 * place + x, c)]
            ag_copy(src, place, c, ax_s.at[0], partner, x).wait_recv()

        ag_sends(t, lambda copy: copy.start())

    def body(t, carry):
        rs_step(t)

        @pl.when(t >= lag)
        def _():
            ag_step(t - lag)

        return carry

    lax.fori_loop(0, steps, body, 0)

    width = acc.shape[1] // 128
    local = acc[:, 0:128]
    for q in range(1, width):
        local = local + acc[:, q * 128 : (q + 1) * 128]

    def norm_copy(k):
        return pltpu.make_async_remote_copy(
            src_ref=nsend.at[k], dst_ref=nrecv.at[k], send_sem=ns_s.at[k],
            recv_sem=nr_s.at[k], device_id=flips[k], device_id_type=MESH,
        )

    nsend[0] = local
    norm_copy(0).start()
    done = 0
    for t in range(lag):
        ag_step(steps - lag + t)
        while done < min(len(flips), (t + 1) * 2):
            norm_copy(done).wait()
            local = nsend[done] + nrecv[done]
            done += 1
            if done < len(flips):
                nsend[done] = local
                norm_copy(done).start()
    while done < len(flips):
        norm_copy(done).wait()
        local = nsend[done] + nrecv[done]
        done += 1
        if done < len(flips):
            nsend[done] = local
            norm_copy(done).start()
    nrm[...] = local

    def drain(t, carry):
        c, place = t // nz, t % nz
        k = c * nz + place
        x_copy(k).wait_send()

        @pl.when(place > z)
        def _():
            z_copy(0, k, above).wait_send()

        @pl.when(place < z)
        def _():
            z_copy(1, k, below).wait_send()

        ag_sends(t, lambda copy: copy.wait_send())
        src = upd.at[shard_rows(2 * place + 1 - x, c)]
        ag_copy(src, place, c, ax_s.at[0], partner, 1 - x).wait_recv()
        return carry

    lax.fori_loop(0, steps, drain, 0)
    for c in range(chunks):
        own_copy(c).wait()


def exchange(nz, nmp, preactivation, upstream, weight, first_moment, second_moment):
    rows, width = first_moment.shape
    part = min(rows, 256)
    chunks = rows // part
    steps = nz * chunks
    flips = (2 * nz).bit_length() - 1 + nmp.bit_length() - 1
    dma = pltpu.SemaphoreType.DMA
    vmem = pl.BlockSpec(memory_space=pltpu.VMEM)
    anyspec = pl.BlockSpec(memory_space=pl.ANY)
    return pl.pallas_call(
        functools.partial(kernel, nz, nmp, chunks, nz),
        out_shape=(
            jax.ShapeDtypeStruct((rows, width), jnp.float32),
            jax.ShapeDtypeStruct(weight.shape, jnp.bfloat16),
            jax.ShapeDtypeStruct((8, 128), jnp.float32),
        ),
        in_specs=[vmem, vmem, anyspec, vmem, vmem],
        out_specs=(vmem, anyspec, vmem),
        scratch_shapes=[
            pltpu.VMEM((steps, part, width), jnp.bfloat16),
            pltpu.VMEM((steps, part, width), jnp.bfloat16),
            pltpu.VMEM((2 * steps, part, width), jnp.bfloat16),
            pltpu.VMEM((rows, width), jnp.bfloat16),
            pltpu.VMEM((rows, width), jnp.bfloat16),
            pltpu.VMEM((8, width), jnp.float32),
            pltpu.VMEM((flips, 8, 128), jnp.float32),
            pltpu.VMEM((flips, 8, 128), jnp.float32),
            dma((steps,)),
            dma((steps,)),
            dma((2 * steps,)),
            dma((2 * steps,)),
            dma((steps,)),
            dma((2 * steps,)),
            dma((2 * steps,)),
            dma((chunks,)),
            dma,
            dma((flips,)),
            dma((flips,)),
        ],
        compiler_params=pltpu.CompilerParams(
            collective_id=0, has_side_effects=True, vmem_limit_bytes=56 * 2**20
        ),
    )(preactivation, upstream, weight, first_moment, second_moment)


def per_device(nz, nmp, preactivation, upstream, weight, first_moment, second_moment):
    owned = first_moment.shape[0]
    gradient, updates, norms = exchange(
        nz, nmp, preactivation, upstream, weight, first_moment, second_moment
    )
    back = lax.dot_general(
        upstream, weight, (((1,), (1,)), ((), ())), preferred_element_type=jnp.float32
    )
    input_grad = jnp.where(preactivation > 0, back, jnp.zeros((), jnp.float32)).astype(jnp.bfloat16)
    start_row = lax.axis_index("dp") * owned
    own_weight = lax.dynamic_slice_in_dim(weight, start_row, owned, 0).astype(jnp.float32)
    first_next, second_next, update = moments(gradient, first_moment, second_moment, own_weight)
    ratio = jnp.sqrt(jnp.sum(norms[0])) / jnp.sqrt(jnp.sum(norms[1]))
    trust_step = ratio * update
    new_weight = (
        weight.astype(jnp.float32) - 0.02 * (ratio * updates.astype(jnp.float32))
    ).astype(jnp.bfloat16)
    return (input_grad, new_weight, first_next, second_next, trust_step)


def solution(mesh):
    return jax.shard_map(
        functools.partial(per_device, mesh.shape["dp"] // 2, mesh.shape["mp"]),
        mesh=mesh,
        in_specs=(
            P("dp", "mp"),
            P("dp", None),
            P("mp", None),
            P(("mp", "dp"), None),
            P(("mp", "dp"), None),
        ),
        out_specs=(
            P("dp", "mp"),
            P("mp", None),
            P(("mp", "dp"), None),
            P(("mp", "dp"), None),
            P(("mp", "dp"), None),
        ),
        check_vma=False,
    )
```

```python
import functools

import jax
import jax.numpy as jnp
from jax import lax
from jax.experimental import pallas as pl
from jax.experimental.pallas import tpu as pltpu
from jax.sharding import PartitionSpec as P

STEP = 1000
BETA_ONE = 0.9
BETA_TWO = 0.999
BIAS_ONE = 1.0 - BETA_ONE**STEP
BIAS_TWO = 1.0 - BETA_TWO**STEP
MESH = pl.DeviceIdType.MESH


def moments(gradient, first_moment, second_moment, own_weight):
    first_next = BETA_ONE * first_moment + (1.0 - BETA_ONE) * gradient
    second_next = BETA_TWO * second_moment + (1.0 - BETA_TWO) * gradient * gradient
    update = first_next / BIAS_ONE / (jnp.sqrt(second_next / BIAS_TWO) + 1e-06) + 0.02 * own_weight
    return first_next, second_next, update


def kernel(
    nz, nmp, chunks, first_rows, lead,
    pre, ups, w_hbm, m, v,
    g_out, upd, nrm,
    xs, xr, qs, qxs, qxr, zb, tb, ub, wv, acc, nsend, nrecv,
    xs_s, xr_s, qs_s, qr_s, zs_s, zr_s, ax_s, az_s, aqx_s, aqz_s,
    arz_s, arx_s, arq_s, own_s, w_s, ns_s, nr_s,
):
    dp = lax.axis_index("dp")
    mp = lax.axis_index("mp")
    z, x = dp // 2, dp % 2
    rows = m.shape[0]
    part = rows // chunks
    rest = part - first_rows
    steps = nz * chunks
    partner = 2 * z + 1 - x
    below, above = dp - 2, dp + 2
    lag = nz + 1

    flips = []
    bit = 1
    while bit < 2 * nz:
        flips.append({"dp": dp + bit * (1 - 2 * ((dp // bit) % 2))})
        bit *= 2
    bit = 1
    while bit < nmp:
        flips.append({"mp": mp + bit * (1 - 2 * ((mp // bit) % 2))})
        bit *= 2

    w_copy = pltpu.make_async_copy(
        w_hbm.at[pl.ds(pl.multiple_of(dp * rows, rows), rows)], wv, w_s
    )
    w_copy.start()

    barrier = pltpu.get_barrier_semaphore()
    for k, device in enumerate(flips):
        if k != 1:
            pl.semaphore_signal(barrier, inc=1, device_id=device, device_id_type=MESH)

    @pl.when(z > 0)
    def _():
        pl.semaphore_signal(barrier, inc=1, device_id={"dp": below}, device_id_type=MESH)

    @pl.when(z < nz - 1)
    def _():
        pl.semaphore_signal(barrier, inc=1, device_id={"dp": above}, device_id_type=MESH)

    ends = jnp.where(z > 0, 1, 0) + jnp.where(z < nz - 1, 1, 0)
    pl.semaphore_wait(barrier, len(flips) - 1 + ends)

    def order(j):
        up, down = nz - 1 - z, z
        short = jnp.minimum(up, down)
        single = nz - 1 - 2 * short
        toward = jnp.where(up >= down, 1, -1)
        t = jnp.maximum(j - single, 0)
        dist = jnp.where(j < single, jnp.maximum(up, down) - j, short - t // 2)
        side = jnp.where(j < single, 1, 1 - 2 * (t % 2))
        return z + toward * side * dist

    def partial_of(dest, column, c):
        at = pl.multiple_of((2 * dest + column) * rows + c * part, part)
        hidden = jnp.maximum(pre[:, pl.ds(at, part)], jnp.zeros((), jnp.bfloat16))
        return lax.dot_general(
            hidden, ups[...], (((0,), (0,)), ((), ())), preferred_element_type=jnp.float32
        )

    def remote(src, dst, send, recv, device):
        return pltpu.make_async_remote_copy(
            src_ref=src, dst_ref=dst, send_sem=send, recv_sem=recv,
            device_id={"dp": device}, device_id_type=MESH,
        )

    def x_copy(k):
        return remote(xs.at[k], xr.at[k], xs_s.at[k], xr_s.at[k], partner)

    def q_copy(c):
        return remote(qxs.at[c], qxr.at[c], qs_s.at[c], qr_s.at[c], partner)

    def z_copy(way, k, device):
        at = way * steps + k
        return remote(zb.at[at], zb.at[at], zs_s.at[at], zr_s.at[at], device)

    def own_rows(c):
        return pl.ds(pl.multiple_of(c * part, part), part)

    def own_first(c):
        return pl.ds(pl.multiple_of(c * part, part), first_rows)

    def own_rest(c):
        return pl.ds(pl.multiple_of(c * part + first_rows, 16), rest)

    def all_of(shard, c):
        return upd.at[pl.ds(pl.multiple_of(shard * rows + c * part, part), part)]

    def first_of(shard, c):
        return upd.at[pl.ds(pl.multiple_of(shard * rows + c * part, part), first_rows)]

    def rest_of(shard, c):
        return upd.at[pl.ds(pl.multiple_of(shard * rows + c * part + first_rows, 16), rest)]

    def own_copy(c):
        return pltpu.make_async_copy(ub.at[own_rows(c)], all_of(dp, c), own_s.at[c])

    def send_x(t):
        c, dest = t // nz, order(t % nz)
        k = c * nz + dest
        total = partial_of(dest, 1 - x, c)
        xs[k] = total[:first_rows].astype(jnp.bfloat16)
        qs[k] = total[first_rows:].astype(jnp.bfloat16)
        x_copy(k).start()

    def rs_step(t):
        c, dest = t // nz, order(t % nz)
        k = c * nz + dest
        tb[0:part] = partial_of(dest, x, c)
        tb[part:] = qs[k].astype(jnp.float32)
        x_copy(k).wait_recv()
        tb[0:first_rows] += xr[k].astype(jnp.float32)

        @pl.when((dest >= z) & (z > 0))
        def _():
            z_copy(0, k, below).wait_recv()
            tb[...] += zb[k].astype(jnp.float32)

        @pl.when((dest <= z) & (z < nz - 1))
        def _():
            z_copy(1, k, above).wait_recv()
            tb[...] += zb[steps + k].astype(jnp.float32)

        @pl.when(dest > z)
        def _():
            zb[k] = tb[...].astype(jnp.bfloat16)
            z_copy(0, k, above).start()

        @pl.when(dest < z)
        def _():
            zb[steps + k] = tb[...].astype(jnp.bfloat16)
            z_copy(1, k, below).start()

        @pl.when(dest == z)
        def _():
            g_out[own_rows(c)] = tb[0:part]
            qxs[c] = tb[part:].astype(jnp.bfloat16)
            q_copy(c).start()

    def finish(c):
        q_copy(c).wait_recv()
        g_out[own_rest(c)] += qxr[c].astype(jnp.float32)
        own_weight = wv[own_rows(c)].astype(jnp.float32)
        _, _, update = moments(g_out[own_rows(c)], m[own_rows(c)], v[own_rows(c)], own_weight)
        ub[own_rows(c)] = update.astype(jnp.bfloat16)
        own_copy(c).start()
        acc[0:1] += jnp.sum(own_weight * own_weight, axis=0, keepdims=True)
        acc[1:2] += jnp.sum(update * update, axis=0, keepdims=True)

    def ag_sends(t, act):
        c, place = t // nz, order(nz - 1 - t % nz)
        k = c * nz + place
        shard = 2 * place + x

        def sends(whole, first):
            @pl.when((place <= z) & (z < nz - 1))
            def _():
                act(remote(whole, all_of(shard, c), az_s.at[k], arz_s.at[k], above))

            @pl.when((place >= z) & (z > 0))
            def _():
                at = steps + k
                act(remote(whole, all_of(shard, c), az_s.at[at], arz_s.at[k], below))

            act(remote(first, first_of(shard, c), ax_s.at[k], arx_s.at[k], partner))

        @pl.when(place == z)
        def _():
            act(
                remote(
                    ub.at[own_rest(c)], rest_of(shard, c), aqx_s.at[c], arq_s.at[k], partner
                )
            )
            sends(ub.at[own_rows(c)], ub.at[own_first(c)])

        @pl.when(place != z)
        def _():
            sends(all_of(shard, c), first_of(shard, c))

    def agq_sends(t, act):
        c, place = t // nz, order(nz - 1 - t % nz)
        k = c * nz + place
        block = rest_of(2 * place + 1 - x, c)

        @pl.when((place <= z) & (z < nz - 1))
        def _():
            act(remote(block, block, aqz_s.at[k], arq_s.at[k], above))

        @pl.when((place >= z) & (z > 0))
        def _():
            act(remote(block, block, aqz_s.at[steps + k], arq_s.at[k], below))

    def ag_step(t):
        c, place = t // nz, order(nz - 1 - t % nz)
        k = c * nz + place

        @pl.when(place != z)
        def _():
            block = all_of(2 * place + x, c)
            remote(block, block, az_s.at[k], arz_s.at[k], partner).wait_recv()

        ag_sends(t, lambda copy: copy.start())

    def agq_step(t):
        c, place = t // nz, order(nz - 1 - t % nz)
        k = c * nz + place
        block = rest_of(2 * place + 1 - x, c)
        remote(block, block, aqz_s.at[k], arq_s.at[k], partner).wait_recv()
        agq_sends(t, lambda copy: copy.start())

    def start_x(t, carry):
        send_x(t)
        return carry

    lax.fori_loop(0, lead, start_x, 0)
    w_copy.wait()
    acc[...] = jnp.zeros_like(acc)

    def body(t, carry):
        @pl.when(t + lead < steps)
        def _():
            send_x(t + lead)

        @pl.when(t < steps)
        def _():
            rs_step(t)

        @pl.when((t >= nz) & (t % nz == 1))
        def _():
            finish(t // nz - 1)

        @pl.when(t >= lag)
        def _():
            ag_step(t - lag)

        @pl.when(t >= lag + 1)
        def _():
            agq_step(t - lag - 1)

        return carry

    lax.fori_loop(0, steps + 2, body, 0)

    width = acc.shape[1] // 128
    local = acc[:, 0:128]
    for q in range(1, width):
        local = local + acc[:, q * 128 : (q + 1) * 128]

    def norm_copy(k):
        return pltpu.make_async_remote_copy(
            src_ref=nsend.at[k], dst_ref=nrecv.at[k], send_sem=ns_s.at[k],
            recv_sem=nr_s.at[k], device_id=flips[k], device_id_type=MESH,
        )

    nsend[0] = local
    norm_copy(0).start()
    done = 0
    for t in range(steps + 2, steps + lag + 1):
        if t - lag < steps:
            ag_step(t - lag)
        agq_step(t - lag - 1)
        for _ in range(2):
            if done < len(flips):
                norm_copy(done).wait()
                local = nsend[done] + nrecv[done]
                done += 1
                if done < len(flips):
                    nsend[done] = local
                    norm_copy(done).start()
    nrm[...] = local

    def drain(t, carry):
        c, place = t // nz, t % nz
        k = c * nz + place
        x_copy(k).wait_send()

        @pl.when(place > z)
        def _():
            z_copy(0, k, above).wait_send()

        @pl.when(place < z)
        def _():
            z_copy(1, k, below).wait_send()

        ag_sends(t, lambda copy: copy.wait_send())
        agq_sends(t, lambda copy: copy.wait_send())
        block = first_of(2 * place + 1 - x, c)
        remote(block, block, ax_s.at[k], arx_s.at[k], partner).wait_recv()
        return carry

    lax.fori_loop(0, steps, drain, 0)
    for c in range(chunks):
        own_copy(c).wait()
        q_copy(c).wait_send()


def exchange(nz, nmp, preactivation, upstream, weight, first_moment, second_moment):
    rows, width = first_moment.shape
    part = min(rows, 256)
    first_rows = part * 5 // 8
    rest = part - first_rows
    chunks = rows // part
    steps = nz * chunks
    flips = (2 * nz).bit_length() - 1 + nmp.bit_length() - 1
    dma = pltpu.SemaphoreType.DMA
    vmem = pl.BlockSpec(memory_space=pltpu.VMEM)
    anyspec = pl.BlockSpec(memory_space=pl.ANY)
    return pl.pallas_call(
        functools.partial(kernel, nz, nmp, chunks, first_rows, min(nz + 2, steps)),
        out_shape=(
            jax.ShapeDtypeStruct((rows, width), jnp.float32),
            jax.ShapeDtypeStruct(weight.shape, jnp.bfloat16),
            jax.ShapeDtypeStruct((8, 128), jnp.float32),
        ),
        in_specs=[vmem, vmem, anyspec, vmem, vmem],
        out_specs=(vmem, anyspec, vmem),
        scratch_shapes=[
            pltpu.VMEM((steps, first_rows, width), jnp.bfloat16),
            pltpu.VMEM((steps, first_rows, width), jnp.bfloat16),
            pltpu.VMEM((steps, rest, width), jnp.bfloat16),
            pltpu.VMEM((chunks, rest, width), jnp.bfloat16),
            pltpu.VMEM((chunks, rest, width), jnp.bfloat16),
            pltpu.VMEM((2 * steps, part + rest, width), jnp.bfloat16),
            pltpu.VMEM((part + rest, width), jnp.float32),
            pltpu.VMEM((rows, width), jnp.bfloat16),
            pltpu.VMEM((rows, width), jnp.bfloat16),
            pltpu.VMEM((8, width), jnp.float32),
            pltpu.VMEM((flips, 8, 128), jnp.float32),
            pltpu.VMEM((flips, 8, 128), jnp.float32),
            dma((steps,)),
            dma((steps,)),
            dma((chunks,)),
            dma((chunks,)),
            dma((2 * steps,)),
            dma((2 * steps,)),
            dma((steps,)),
            dma((2 * steps,)),
            dma((chunks,)),
            dma((2 * steps,)),
            dma((steps,)),
            dma((steps,)),
            dma((steps,)),
            dma((chunks,)),
            dma,
            dma((flips,)),
            dma((flips,)),
        ],
        compiler_params=pltpu.CompilerParams(
            collective_id=0, has_side_effects=True, vmem_limit_bytes=56 * 2**20
        ),
    )(preactivation, upstream, weight, first_moment, second_moment)


def per_device(nz, nmp, preactivation, upstream, weight, first_moment, second_moment):
    owned = first_moment.shape[0]
    gradient, updates, norms = exchange(
        nz, nmp, preactivation, upstream, weight, first_moment, second_moment
    )
    back = lax.dot_general(
        upstream, weight, (((1,), (1,)), ((), ())), preferred_element_type=jnp.float32
    )
    input_grad = jnp.where(preactivation > 0, back, jnp.zeros((), jnp.float32)).astype(jnp.bfloat16)
    start_row = lax.axis_index("dp") * owned
    own_weight = lax.dynamic_slice_in_dim(weight, start_row, owned, 0).astype(jnp.float32)
    first_next, second_next, update = moments(gradient, first_moment, second_moment, own_weight)
    ratio = jnp.sqrt(jnp.sum(norms[0])) / jnp.sqrt(jnp.sum(norms[1]))
    trust_step = ratio * update
    new_weight = (
        weight.astype(jnp.float32) - 0.02 * (ratio * updates.astype(jnp.float32))
    ).astype(jnp.bfloat16)
    return (input_grad, new_weight, first_next, second_next, trust_step)


def solution(mesh):
    return jax.shard_map(
        functools.partial(per_device, mesh.shape["dp"] // 2, mesh.shape["mp"]),
        mesh=mesh,
        in_specs=(
            P("dp", "mp"),
            P("dp", None),
            P("mp", None),
            P(("mp", "dp"), None),
            P(("mp", "dp"), None),
        ),
        out_specs=(
            P("dp", "mp"),
            P("mp", None),
            P(("mp", "dp"), None),
            P(("mp", "dp"), None),
            P(("mp", "dp"), None),
        ),
        check_vma=False,
    )
```

```python
import functools

import jax
import jax.numpy as jnp
from jax import lax
from jax.experimental import pallas as pl
from jax.experimental.pallas import tpu as pltpu
from jax.sharding import PartitionSpec as P

STEP = 1000
BETA_ONE = 0.9
BETA_TWO = 0.999
BIAS_ONE = 1.0 - BETA_ONE**STEP
BIAS_TWO = 1.0 - BETA_TWO**STEP
MESH = pl.DeviceIdType.MESH


def moments(gradient, first_moment, second_moment, own_weight):
    first_next = BETA_ONE * first_moment + (1.0 - BETA_ONE) * gradient
    second_next = BETA_TWO * second_moment + (1.0 - BETA_TWO) * gradient * gradient
    update = first_next / BIAS_ONE / (jnp.sqrt(second_next / BIAS_TWO) + 1e-06) + 0.02 * own_weight
    return first_next, second_next, update


def kernel(
    nz, nmp, chunks, first_rows, lead,
    pre, ups, w_hbm, m, v,
    g_out, upd, nrm,
    xs, xr, qs, qxs, qxr, zb, tb, ub, wv, acc, nsend, nrecv,
    xs_s, xr_s, qs_s, qr_s, zs_s, zr_s, ax_s, az_s, aqx_s, aqz_s,
    arz_s, arx_s, arq_s, own_s, w_s, ns_s, nr_s,
):
    dp = lax.axis_index("dp")
    mp = lax.axis_index("mp")
    z, x = dp // 2, dp % 2
    rows = m.shape[0]
    part = rows // chunks
    rest = part - first_rows
    steps = nz * chunks
    partner = 2 * z + 1 - x
    below, above = dp - 2, dp + 2
    lag = 2 * nz + 1

    flips = []
    bit = 1
    while bit < 2 * nz:
        flips.append({"dp": dp + bit * (1 - 2 * ((dp // bit) % 2))})
        bit *= 2
    bit = 1
    while bit < nmp:
        flips.append({"mp": mp + bit * (1 - 2 * ((mp // bit) % 2))})
        bit *= 2

    w_copy = pltpu.make_async_copy(
        w_hbm.at[pl.ds(pl.multiple_of(dp * rows, rows), rows)], wv, w_s
    )
    w_copy.start()

    barrier = pltpu.get_barrier_semaphore()
    for k, device in enumerate(flips):
        if k != 1:
            pl.semaphore_signal(barrier, inc=1, device_id=device, device_id_type=MESH)

    @pl.when(z > 0)
    def _():
        pl.semaphore_signal(barrier, inc=1, device_id={"dp": below}, device_id_type=MESH)

    @pl.when(z < nz - 1)
    def _():
        pl.semaphore_signal(barrier, inc=1, device_id={"dp": above}, device_id_type=MESH)

    ends = jnp.where(z > 0, 1, 0) + jnp.where(z < nz - 1, 1, 0)
    pl.semaphore_wait(barrier, len(flips) - 1 + ends)

    def order(j):
        up, down = nz - 1 - z, z
        short = jnp.minimum(up, down)
        single = nz - 1 - 2 * short
        toward = jnp.where(up >= down, 1, -1)
        t = jnp.maximum(j - single, 0)
        dist = jnp.where(j < single, jnp.maximum(up, down) - j, short - t // 2)
        side = jnp.where(j < single, 1, 1 - 2 * (t % 2))
        return z + toward * side * dist

    def partial_of(dest, column, c):
        at = pl.multiple_of((2 * dest + column) * rows + c * part, part)
        hidden = jnp.maximum(pre[:, pl.ds(at, part)], jnp.zeros((), jnp.bfloat16))
        return lax.dot_general(
            hidden, ups[...], (((0,), (0,)), ((), ())), preferred_element_type=jnp.float32
        )

    def remote(src, dst, send, recv, device):
        return pltpu.make_async_remote_copy(
            src_ref=src, dst_ref=dst, send_sem=send, recv_sem=recv,
            device_id={"dp": device}, device_id_type=MESH,
        )

    def x_copy(k):
        return remote(xs.at[k], xr.at[k], xs_s.at[k], xr_s.at[k], partner)

    def q_copy(c):
        return remote(qxs.at[c], qxr.at[c], qs_s.at[c], qr_s.at[c], partner)

    def z_copy(way, k, device):
        at = way * steps + k
        return remote(zb.at[at], zb.at[at], zs_s.at[at], zr_s.at[at], device)

    def own_rows(c):
        return pl.ds(pl.multiple_of(c * part, part), part)

    def own_first(c):
        return pl.ds(pl.multiple_of(c * part, part), first_rows)

    def own_rest(c):
        return pl.ds(pl.multiple_of(c * part + first_rows, 16), rest)

    def all_of(shard, c):
        return upd.at[pl.ds(pl.multiple_of(shard * rows + c * part, part), part)]

    def first_of(shard, c):
        return upd.at[pl.ds(pl.multiple_of(shard * rows + c * part, part), first_rows)]

    def rest_of(shard, c):
        return upd.at[pl.ds(pl.multiple_of(shard * rows + c * part + first_rows, 16), rest)]

    def own_copy(c):
        return pltpu.make_async_copy(ub.at[own_rows(c)], all_of(dp, c), own_s.at[c])

    def send_x(t):
        c, dest = t // nz, order(t % nz)
        k = c * nz + dest
        total = partial_of(dest, 1 - x, c)
        xs[k] = total[:first_rows].astype(jnp.bfloat16)
        qs[k] = total[first_rows:].astype(jnp.bfloat16)
        x_copy(k).start()

    def rs_step(t):
        c, dest = t // nz, order(t % nz)
        k = c * nz + dest
        tb[0:part] = partial_of(dest, x, c)
        tb[part:] = qs[k].astype(jnp.float32)
        x_copy(k).wait_recv()
        tb[0:first_rows] += xr[k].astype(jnp.float32)

        @pl.when((dest >= z) & (z > 0))
        def _():
            z_copy(0, k, below).wait_recv()
            tb[...] += zb[k].astype(jnp.float32)

        @pl.when((dest <= z) & (z < nz - 1))
        def _():
            z_copy(1, k, above).wait_recv()
            tb[...] += zb[steps + k].astype(jnp.float32)

        @pl.when(dest > z)
        def _():
            zb[k] = tb[...].astype(jnp.bfloat16)
            z_copy(0, k, above).start()

        @pl.when(dest < z)
        def _():
            zb[steps + k] = tb[...].astype(jnp.bfloat16)
            z_copy(1, k, below).start()

        @pl.when(dest == z)
        def _():
            g_out[own_rows(c)] = tb[0:part]
            qxs[c] = tb[part:].astype(jnp.bfloat16)
            q_copy(c).start()

    def finish(c):
        q_copy(c).wait_recv()
        g_out[own_rest(c)] += qxr[c].astype(jnp.float32)
        own_weight = wv[own_rows(c)].astype(jnp.float32)
        _, _, update = moments(g_out[own_rows(c)], m[own_rows(c)], v[own_rows(c)], own_weight)
        ub[own_rows(c)] = update.astype(jnp.bfloat16)
        own_copy(c).start()
        acc[0:1] += jnp.sum(own_weight * own_weight, axis=0, keepdims=True)
        acc[1:2] += jnp.sum(update * update, axis=0, keepdims=True)

    def ag_sends(t, act):
        c, place = t // nz, order(nz - 1 - t % nz)
        k = c * nz + place
        shard = 2 * place + x

        def sends(whole, first):
            @pl.when((place <= z) & (z < nz - 1))
            def _():
                act(remote(whole, all_of(shard, c), az_s.at[k], arz_s.at[k], above))

            @pl.when((place >= z) & (z > 0))
            def _():
                at = steps + k
                act(remote(whole, all_of(shard, c), az_s.at[at], arz_s.at[k], below))

            act(remote(first, first_of(shard, c), ax_s.at[k], arx_s.at[k], partner))

        @pl.when(place == z)
        def _():
            act(
                remote(
                    ub.at[own_rest(c)], rest_of(shard, c), aqx_s.at[c], arq_s.at[k], partner
                )
            )
            sends(ub.at[own_rows(c)], ub.at[own_first(c)])

        @pl.when(place != z)
        def _():
            sends(all_of(shard, c), first_of(shard, c))

    def agq_sends(t, act):
        c, place = t // nz, order(nz - 1 - t % nz)
        k = c * nz + place
        block = rest_of(2 * place + 1 - x, c)

        @pl.when((place <= z) & (z < nz - 1))
        def _():
            act(remote(block, block, aqz_s.at[k], arq_s.at[k], above))

        @pl.when((place >= z) & (z > 0))
        def _():
            act(remote(block, block, aqz_s.at[steps + k], arq_s.at[k], below))

    def ag_step(t):
        c, place = t // nz, order(nz - 1 - t % nz)
        k = c * nz + place

        @pl.when(place != z)
        def _():
            block = all_of(2 * place + x, c)
            remote(block, block, az_s.at[k], arz_s.at[k], partner).wait_recv()

        ag_sends(t, lambda copy: copy.start())

    def agq_step(t):
        c, place = t // nz, order(nz - 1 - t % nz)
        k = c * nz + place
        block = rest_of(2 * place + 1 - x, c)
        remote(block, block, aqz_s.at[k], arq_s.at[k], partner).wait_recv()
        agq_sends(t, lambda copy: copy.start())

    def start_x(t, carry):
        send_x(t)
        return carry

    lax.fori_loop(0, lead, start_x, 0)
    w_copy.wait()
    acc[...] = jnp.zeros_like(acc)

    def norm_copy(k):
        return pltpu.make_async_remote_copy(
            src_ref=nsend.at[k], dst_ref=nrecv.at[k], send_sem=ns_s.at[k],
            recv_sem=nr_s.at[k], device_id=flips[k], device_id_type=MESH,
        )

    def norm_step(k):
        if k == 0:
            local = acc[:, 0:128]
            for q in range(1, acc.shape[1] // 128):
                local = local + acc[:, q * 128 : (q + 1) * 128]
        else:
            norm_copy(k - 1).wait()
            local = nsend[k - 1] + nrecv[k - 1]
        if k < len(flips):
            nsend[k] = local
            norm_copy(k).start()
        else:
            nrm[...] = local

    last = steps + nz * ((nz - 1) // 2)
    norm_at = steps + nz + 2

    def late(u, act):
        j = u % nz
        c = u // nz - j // 2

        @pl.when((u >= 0) & (c >= 0) & (c < chunks))
        def _():
            act(c * nz + j)

    def body(t, carry):
        @pl.when(t + lead < steps)
        def _():
            send_x(t + lead)

        @pl.when((t < steps) & (t % nz != nz - 1))
        def _():
            rs_step(t)

        @pl.when((t >= nz) & (t < steps + nz) & (t % nz == nz - 1))
        def _():
            rs_step(t - nz)

        @pl.when((t >= 2 * nz) & (t < steps + 2 * nz) & (t % nz == 1))
        def _():
            finish(t // nz - 2)

        late(t - lag, ag_step)
        late(t - lag - 2, agq_step)
        for k in range(len(flips)):

            @pl.when(t == norm_at + k)
            def _():
                norm_step(k)

        return carry

    lax.fori_loop(0, last + lag + 2, body, 0)
    norm_step(len(flips))

    def drain(t, carry):
        c, place = t // nz, t % nz
        k = c * nz + place
        x_copy(k).wait_send()

        @pl.when(place > z)
        def _():
            z_copy(0, k, above).wait_send()

        @pl.when(place < z)
        def _():
            z_copy(1, k, below).wait_send()

        ag_sends(t, lambda copy: copy.wait_send())
        agq_sends(t, lambda copy: copy.wait_send())
        block = first_of(2 * place + 1 - x, c)
        remote(block, block, ax_s.at[k], arx_s.at[k], partner).wait_recv()
        return carry

    lax.fori_loop(0, steps, drain, 0)
    for c in range(chunks):
        own_copy(c).wait()
        q_copy(c).wait_send()


def exchange(nz, nmp, preactivation, upstream, weight, first_moment, second_moment):
    rows, width = first_moment.shape
    part = min(rows, 128)
    first_rows = part * 5 // 8
    rest = part - first_rows
    chunks = rows // part
    steps = nz * chunks
    flips = (2 * nz).bit_length() - 1 + nmp.bit_length() - 1
    dma = pltpu.SemaphoreType.DMA
    vmem = pl.BlockSpec(memory_space=pltpu.VMEM)
    anyspec = pl.BlockSpec(memory_space=pl.ANY)
    return pl.pallas_call(
        functools.partial(kernel, nz, nmp, chunks, first_rows, min(2 * nz, steps)),
        out_shape=(
            jax.ShapeDtypeStruct((rows, width), jnp.float32),
            jax.ShapeDtypeStruct(weight.shape, jnp.bfloat16),
            jax.ShapeDtypeStruct((8, 128), jnp.float32),
        ),
        in_specs=[vmem, vmem, anyspec, vmem, vmem],
        out_specs=(vmem, anyspec, vmem),
        scratch_shapes=[
            pltpu.VMEM((steps, first_rows, width), jnp.bfloat16),
            pltpu.VMEM((steps, first_rows, width), jnp.bfloat16),
            pltpu.VMEM((steps, rest, width), jnp.bfloat16),
            pltpu.VMEM((chunks, rest, width), jnp.bfloat16),
            pltpu.VMEM((chunks, rest, width), jnp.bfloat16),
            pltpu.VMEM((2 * steps, part + rest, width), jnp.bfloat16),
            pltpu.VMEM((part + rest, width), jnp.float32),
            pltpu.VMEM((rows, width), jnp.bfloat16),
            pltpu.VMEM((rows, width), jnp.bfloat16),
            pltpu.VMEM((8, width), jnp.float32),
            pltpu.VMEM((flips, 8, 128), jnp.float32),
            pltpu.VMEM((flips, 8, 128), jnp.float32),
            dma((steps,)),
            dma((steps,)),
            dma((chunks,)),
            dma((chunks,)),
            dma((2 * steps,)),
            dma((2 * steps,)),
            dma((steps,)),
            dma((2 * steps,)),
            dma((chunks,)),
            dma((2 * steps,)),
            dma((steps,)),
            dma((steps,)),
            dma((steps,)),
            dma((chunks,)),
            dma,
            dma((flips,)),
            dma((flips,)),
        ],
        compiler_params=pltpu.CompilerParams(
            collective_id=0, has_side_effects=True, vmem_limit_bytes=56 * 2**20
        ),
    )(preactivation, upstream, weight, first_moment, second_moment)


def per_device(nz, nmp, preactivation, upstream, weight, first_moment, second_moment):
    owned = first_moment.shape[0]
    gradient, updates, norms = exchange(
        nz, nmp, preactivation, upstream, weight, first_moment, second_moment
    )
    back = lax.dot_general(
        upstream, weight, (((1,), (1,)), ((), ())), preferred_element_type=jnp.float32
    )
    input_grad = jnp.where(preactivation > 0, back, jnp.zeros((), jnp.float32)).astype(jnp.bfloat16)
    start_row = lax.axis_index("dp") * owned
    own_weight = lax.dynamic_slice_in_dim(weight, start_row, owned, 0).astype(jnp.float32)
    first_next, second_next, update = moments(gradient, first_moment, second_moment, own_weight)
    ratio = jnp.sqrt(jnp.sum(norms[0])) / jnp.sqrt(jnp.sum(norms[1]))
    trust_step = ratio * update
    new_weight = (
        weight.astype(jnp.float32) - 0.02 * (ratio * updates.astype(jnp.float32))
    ).astype(jnp.bfloat16)
    return (input_grad, new_weight, first_next, second_next, trust_step)


def solution(mesh):
    return jax.shard_map(
        functools.partial(per_device, mesh.shape["dp"] // 2, mesh.shape["mp"]),
        mesh=mesh,
        in_specs=(
            P("dp", "mp"),
            P("dp", None),
            P("mp", None),
            P(("mp", "dp"), None),
            P(("mp", "dp"), None),
        ),
        out_specs=(
            P("dp", "mp"),
            P("mp", None),
            P(("mp", "dp"), None),
            P(("mp", "dp"), None),
            P(("mp", "dp"), None),
        ),
        check_vma=False,
    )
```

```python
import functools

import jax
import jax.numpy as jnp
from jax import lax
from jax.experimental import pallas as pl
from jax.experimental.pallas import tpu as pltpu
from jax.sharding import PartitionSpec as P

STEP = 1000
BETA_ONE = 0.9
BETA_TWO = 0.999
BIAS_ONE = 1.0 - BETA_ONE**STEP
BIAS_TWO = 1.0 - BETA_TWO**STEP
MESH = pl.DeviceIdType.MESH


def moments(gradient, first_moment, second_moment, own_weight):
    first_next = BETA_ONE * first_moment + (1.0 - BETA_ONE) * gradient
    second_next = BETA_TWO * second_moment + (1.0 - BETA_TWO) * gradient * gradient
    update = first_next / BIAS_ONE / (jnp.sqrt(second_next / BIAS_TWO) + 1e-06) + 0.02 * own_weight
    return first_next, second_next, update


def kernel(
    nz, nmp, chunks, first_rows, lead,
    pre, ups, w_hbm, m, v,
    g_out, upd, nrm,
    xs, xr, qs, qxs, qxr, zb, tb, ub, wv, acc, nsend, nrecv,
    xs_s, xr_s, qs_s, qr_s, zs_s, zr_s, ax_s, az_s, aqx_s, aqz_s,
    arz_s, arx_s, arq_s, own_s, w_s, ns_s, nr_s,
):
    dp = lax.axis_index("dp")
    mp = lax.axis_index("mp")
    z, x = dp // 2, dp % 2
    rows = m.shape[0]
    part = rows // chunks
    rest = part - first_rows
    steps = nz * chunks
    partner = 2 * z + 1 - x
    below, above = dp - 2, dp + 2
    lag = nz

    flips = []
    bit = 1
    while bit < 2 * nz:
        flips.append({"dp": dp + bit * (1 - 2 * ((dp // bit) % 2))})
        bit *= 2
    bit = 1
    while bit < nmp:
        flips.append({"mp": mp + bit * (1 - 2 * ((mp // bit) % 2))})
        bit *= 2

    w_copy = pltpu.make_async_copy(
        w_hbm.at[pl.ds(pl.multiple_of(dp * rows, rows), rows)], wv, w_s
    )
    w_copy.start()

    barrier = pltpu.get_barrier_semaphore()
    for k, device in enumerate(flips):
        if k != 1:
            pl.semaphore_signal(barrier, inc=1, device_id=device, device_id_type=MESH)

    @pl.when(z > 0)
    def _():
        pl.semaphore_signal(barrier, inc=1, device_id={"dp": below}, device_id_type=MESH)

    @pl.when(z < nz - 1)
    def _():
        pl.semaphore_signal(barrier, inc=1, device_id={"dp": above}, device_id_type=MESH)

    ends = jnp.where(z > 0, 1, 0) + jnp.where(z < nz - 1, 1, 0)
    pl.semaphore_wait(barrier, len(flips) - 1 + ends)

    def order(j):
        up, down = nz - 1 - z, z
        short = jnp.minimum(up, down)
        single = nz - 1 - 2 * short
        toward = jnp.where(up >= down, 1, -1)
        t = jnp.maximum(j - single, 0)
        dist = jnp.where(j < single, jnp.maximum(up, down) - j, short - t // 2)
        side = jnp.where(j < single, 1, 1 - 2 * (t % 2))
        return z + toward * side * dist

    def partial_of(dest, column, c):
        at = pl.multiple_of((2 * dest + column) * rows + c * part, part)
        hidden = jnp.maximum(pre[:, pl.ds(at, part)], jnp.zeros((), jnp.bfloat16))
        return lax.dot_general(
            hidden, ups[...], (((0,), (0,)), ((), ())), preferred_element_type=jnp.float32
        )

    def remote(src, dst, send, recv, device):
        return pltpu.make_async_remote_copy(
            src_ref=src, dst_ref=dst, send_sem=send, recv_sem=recv,
            device_id={"dp": device}, device_id_type=MESH,
        )

    def x_copy(k):
        return remote(xs.at[k], xr.at[k], xs_s.at[k], xr_s.at[k], partner)

    def q_copy(c):
        return remote(qxs.at[c], qxr.at[c], qs_s.at[c], qr_s.at[c], partner)

    def z_copy(way, k, device):
        at = way * steps + k
        return remote(zb.at[at], zb.at[at], zs_s.at[at], zr_s.at[at], device)

    def own_rows(c):
        return pl.ds(pl.multiple_of(c * part, part), part)

    def own_first(c):
        return pl.ds(pl.multiple_of(c * part, part), first_rows)

    def own_rest(c):
        return pl.ds(pl.multiple_of(c * part + first_rows, 16), rest)

    def all_of(shard, c):
        return upd.at[pl.ds(pl.multiple_of(shard * rows + c * part, part), part)]

    def first_of(shard, c):
        return upd.at[pl.ds(pl.multiple_of(shard * rows + c * part, part), first_rows)]

    def rest_of(shard, c):
        return upd.at[pl.ds(pl.multiple_of(shard * rows + c * part + first_rows, 16), rest)]

    def own_copy(c):
        return pltpu.make_async_copy(ub.at[own_rows(c)], all_of(dp, c), own_s.at[c])

    def send_x(t):
        c, dest = t // nz, order(t % nz)
        k = c * nz + dest
        total = partial_of(dest, 1 - x, c)
        xs[k] = total[:first_rows].astype(jnp.bfloat16)
        qs[k] = total[first_rows:].astype(jnp.bfloat16)
        x_copy(k).start()

    def rs_step(t):
        c, dest = t // nz, order(t % nz)
        k = c * nz + dest
        tb[0:part] = partial_of(dest, x, c)
        tb[part:] = qs[k].astype(jnp.float32)
        x_copy(k).wait_recv()
        tb[0:first_rows] += xr[k].astype(jnp.float32)

        @pl.when((dest >= z) & (z > 0))
        def _():
            z_copy(0, k, below).wait_recv()
            tb[...] += zb[k].astype(jnp.float32)

        @pl.when((dest <= z) & (z < nz - 1))
        def _():
            z_copy(1, k, above).wait_recv()
            tb[...] += zb[steps + k].astype(jnp.float32)

        @pl.when(dest > z)
        def _():
            zb[k] = tb[...].astype(jnp.bfloat16)
            z_copy(0, k, above).start()

        @pl.when(dest < z)
        def _():
            zb[steps + k] = tb[...].astype(jnp.bfloat16)
            z_copy(1, k, below).start()

        @pl.when(dest == z)
        def _():
            g_out[own_rows(c)] = tb[0:part]
            qxs[c] = tb[part:].astype(jnp.bfloat16)
            q_copy(c).start()

    def finish(c):
        q_copy(c).wait_recv()
        g_out[own_rest(c)] += qxr[c].astype(jnp.float32)
        own_weight = wv[own_rows(c)].astype(jnp.float32)
        _, _, update = moments(g_out[own_rows(c)], m[own_rows(c)], v[own_rows(c)], own_weight)
        ub[own_rows(c)] = update.astype(jnp.bfloat16)
        own_copy(c).start()
        acc[0:1] += jnp.sum(own_weight * own_weight, axis=0, keepdims=True)
        acc[1:2] += jnp.sum(update * update, axis=0, keepdims=True)

    def ag_sends(t, act):
        c, place = t // nz, order(nz - 1 - t % nz)
        k = c * nz + place
        shard = 2 * place + x

        def sends(whole, first):
            @pl.when((place <= z) & (z < nz - 1))
            def _():
                act(remote(whole, all_of(shard, c), az_s.at[k], arz_s.at[k], above))

            @pl.when((place >= z) & (z > 0))
            def _():
                at = steps + k
                act(remote(whole, all_of(shard, c), az_s.at[at], arz_s.at[k], below))

            act(remote(first, first_of(shard, c), ax_s.at[k], arx_s.at[k], partner))

        @pl.when(place == z)
        def _():
            act(
                remote(
                    ub.at[own_rest(c)], rest_of(shard, c), aqx_s.at[c], arq_s.at[k], partner
                )
            )
            sends(ub.at[own_rows(c)], ub.at[own_first(c)])

        @pl.when(place != z)
        def _():
            sends(all_of(shard, c), first_of(shard, c))

    def agq_sends(t, act):
        c, place = t // nz, order(nz - 1 - t % nz)
        k = c * nz + place
        block = rest_of(2 * place + 1 - x, c)

        @pl.when((place <= z) & (z < nz - 1))
        def _():
            act(remote(block, block, aqz_s.at[k], arq_s.at[k], above))

        @pl.when((place >= z) & (z > 0))
        def _():
            act(remote(block, block, aqz_s.at[steps + k], arq_s.at[k], below))

    def ag_step(t):
        c, place = t // nz, order(nz - 1 - t % nz)
        k = c * nz + place

        @pl.when(place != z)
        def _():
            block = all_of(2 * place + x, c)
            remote(block, block, az_s.at[k], arz_s.at[k], partner).wait_recv()

        ag_sends(t, lambda copy: copy.start())

    def agq_step(t):
        c, place = t // nz, order(nz - 1 - t % nz)
        k = c * nz + place
        block = rest_of(2 * place + 1 - x, c)
        remote(block, block, aqz_s.at[k], arq_s.at[k], partner).wait_recv()
        agq_sends(t, lambda copy: copy.start())

    def start_x(t, carry):
        send_x(t)
        return carry

    lax.fori_loop(0, lead, start_x, 0)
    w_copy.wait()
    acc[...] = jnp.zeros_like(acc)

    def body(t, carry):
        @pl.when(t + lead < steps)
        def _():
            send_x(t + lead)

        @pl.when(t < steps)
        def _():
            rs_step(t)

        @pl.when((t >= nz) & (t % nz == 0))
        def _():
            finish(t // nz - 1)

        @pl.when(t >= lag)
        def _():
            ag_step(t - lag)

        @pl.when(t >= lag + 1)
        def _():
            agq_step(t - lag - 1)

        return carry

    lax.fori_loop(0, steps + 1, body, 0)

    width = acc.shape[1] // 128
    local = acc[:, 0:128]
    for q in range(1, width):
        local = local + acc[:, q * 128 : (q + 1) * 128]

    def norm_copy(k):
        return pltpu.make_async_remote_copy(
            src_ref=nsend.at[k], dst_ref=nrecv.at[k], send_sem=ns_s.at[k],
            recv_sem=nr_s.at[k], device_id=flips[k], device_id_type=MESH,
        )

    nsend[0] = local
    norm_copy(0).start()
    done = 0
    for t in range(steps + 1, steps + lag + 1):
        if t - lag < steps:
            ag_step(t - lag)
        agq_step(t - lag - 1)
        for _ in range(2):
            if done < len(flips):
                norm_copy(done).wait()
                local = nsend[done] + nrecv[done]
                done += 1
                if done < len(flips):
                    nsend[done] = local
                    norm_copy(done).start()
    weight_sq = jnp.sum(local[0:1], axis=1, keepdims=True)
    update_sq = jnp.sum(local[1:2], axis=1, keepdims=True)
    nrm[...] = jnp.broadcast_to(jnp.sqrt(weight_sq) / jnp.sqrt(update_sq), nrm.shape)

    def drain(t, carry):
        c, place = t // nz, t % nz
        k = c * nz + place
        x_copy(k).wait_send()

        @pl.when(place > z)
        def _():
            z_copy(0, k, above).wait_send()

        @pl.when(place < z)
        def _():
            z_copy(1, k, below).wait_send()

        ag_sends(t, lambda copy: copy.wait_send())
        agq_sends(t, lambda copy: copy.wait_send())
        block = first_of(2 * place + 1 - x, c)
        remote(block, block, ax_s.at[k], arx_s.at[k], partner).wait_recv()
        return carry

    lax.fori_loop(0, steps, drain, 0)
    for c in range(chunks):
        own_copy(c).wait()
        q_copy(c).wait_send()


def exchange(nz, nmp, preactivation, upstream, weight, first_moment, second_moment):
    rows, width = first_moment.shape
    part = min(rows, 256)
    first_rows = part * 13 // 16
    rest = part - first_rows
    chunks = rows // part
    steps = nz * chunks
    flips = (2 * nz).bit_length() - 1 + nmp.bit_length() - 1
    dma = pltpu.SemaphoreType.DMA
    vmem = pl.BlockSpec(memory_space=pltpu.VMEM)
    anyspec = pl.BlockSpec(memory_space=pl.ANY)
    return pl.pallas_call(
        functools.partial(kernel, nz, nmp, chunks, first_rows, min(nz, steps)),
        out_shape=(
            jax.ShapeDtypeStruct((rows, width), jnp.float32),
            jax.ShapeDtypeStruct(weight.shape, jnp.bfloat16),
            jax.ShapeDtypeStruct((8, 128), jnp.float32),
        ),
        in_specs=[vmem, vmem, anyspec, vmem, vmem],
        out_specs=(vmem, anyspec, vmem),
        scratch_shapes=[
            pltpu.VMEM((steps, first_rows, width), jnp.bfloat16),
            pltpu.VMEM((steps, first_rows, width), jnp.bfloat16),
            pltpu.VMEM((steps, rest, width), jnp.bfloat16),
            pltpu.VMEM((chunks, rest, width), jnp.bfloat16),
            pltpu.VMEM((chunks, rest, width), jnp.bfloat16),
            pltpu.VMEM((2 * steps, part + rest, width), jnp.bfloat16),
            pltpu.VMEM((part + rest, width), jnp.float32),
            pltpu.VMEM((rows, width), jnp.bfloat16),
            pltpu.VMEM((rows, width), jnp.bfloat16),
            pltpu.VMEM((8, width), jnp.float32),
            pltpu.VMEM((flips, 8, 128), jnp.float32),
            pltpu.VMEM((flips, 8, 128), jnp.float32),
            dma((steps,)),
            dma((steps,)),
            dma((chunks,)),
            dma((chunks,)),
            dma((2 * steps,)),
            dma((2 * steps,)),
            dma((steps,)),
            dma((2 * steps,)),
            dma((chunks,)),
            dma((2 * steps,)),
            dma((steps,)),
            dma((steps,)),
            dma((steps,)),
            dma((chunks,)),
            dma,
            dma((flips,)),
            dma((flips,)),
        ],
        compiler_params=pltpu.CompilerParams(
            collective_id=0, has_side_effects=True, vmem_limit_bytes=56 * 2**20
        ),
    )(preactivation, upstream, weight, first_moment, second_moment)


def per_device(nz, nmp, preactivation, upstream, weight, first_moment, second_moment):
    owned = first_moment.shape[0]
    gradient, updates, norms = exchange(
        nz, nmp, preactivation, upstream, weight, first_moment, second_moment
    )
    back = lax.dot_general(
        upstream, weight, (((1,), (1,)), ((), ())), preferred_element_type=jnp.float32
    )
    input_grad = jnp.where(preactivation > 0, back, jnp.zeros((), jnp.float32)).astype(jnp.bfloat16)
    start_row = lax.axis_index("dp") * owned
    own_weight = lax.dynamic_slice_in_dim(weight, start_row, owned, 0).astype(jnp.float32)
    first_next, second_next, update = moments(gradient, first_moment, second_moment, own_weight)
    ratio = norms[0, 0]
    trust_step = ratio * update
    new_weight = (
        weight.astype(jnp.float32) - 0.02 * (ratio * updates.astype(jnp.float32))
    ).astype(jnp.bfloat16)
    return (input_grad, new_weight, first_next, second_next, trust_step)


def solution(mesh):
    return jax.shard_map(
        functools.partial(per_device, mesh.shape["dp"] // 2, mesh.shape["mp"]),
        mesh=mesh,
        in_specs=(
            P("dp", "mp"),
            P("dp", None),
            P("mp", None),
            P(("mp", "dp"), None),
            P(("mp", "dp"), None),
        ),
        out_specs=(
            P("dp", "mp"),
            P("mp", None),
            P(("mp", "dp"), None),
            P(("mp", "dp"), None),
            P(("mp", "dp"), None),
        ),
        check_vma=False,
    )
```
